256 devices in a mesh: row: 32 (over z, x), col: 8 (over y, core).
Axes of the slice: x: 4, y: 4, z: 8, core: 2. Of those that a mesh axis runs over, the one named last changes fastest.
Arguments:
- u_panel: bfloat16 [64, 128, 2560], P('row', None, 'col'), may hold values from -6 to 6
- v_panel: bfloat16 [64, 128, 2560], P('row', None, 'col'), may hold values from -0.125 to 0.125
- ranks: int32 [64], P('row'), may hold values from 42 to 128
- inverse_t: float32 [2560, 2560], P('row', 'col'), may hold values from -1 to 2, as said below
Outputs:
- panel_v: bfloat16 [64, 128, 2560], P('row', None, 'col')
- update_left: bfloat16 [64, 8, 8, 128, 2560], P('row', 'col')
The draws below stay inside these ranges and needn't reach their ends.
Inputs may be any that keep to these rules, and one draw needn't show every extreme that they name: inverse_t is upper triangular with its diagonal between 1 and 2.
All inputs are finite; a program needn't handle non-finite values.
Results may differ from the reference program's by a relative error of at most 0.006.
Values may be sent and summed in bfloat16 or wider, within the bound.
No kernel may reach another device: no remote copies, remote signals or barrier semaphores. Data moves between devices by JAX's collectives and lax.ppermute only.
A program may use at most 64 MiB of HBM per device.

```python
import jax
import jax.numpy as jnp
from jax import lax

NB = 2560
K = 128
TPD = 2
NT = 64
JD = 8
N_COL = 8


def draw_inverse_t(key, part):
    key = jax.random.fold_in(key, 7)
    key_off, key_diag = jax.random.split(key)
    offdiag = jax.random.normal(key_off, (NB, NB), jnp.float32)
    offdiag = offdiag * (0.8 / NB ** 0.5)
    diagonal = jax.random.uniform(key_diag, (NB,), jnp.float32, 1.0, 2.0)
    positions = jnp.arange(NB, dtype=jnp.int32)
    above_diag = positions[:, None] < positions[None, :]
    on_diag = positions[:, None] == positions[None, :]
    return jnp.where(above_diag, offdiag, 0.0) + jnp.where(on_diag, diagonal[None, :], 0.0)


def place_ends(values, rng, low, high):
    dims = values.shape
    place = [jax.random.randint(jax.random.fold_in(rng, axis), (), 0, dims[axis]) for axis in range(len(dims))]
    values = values.at[tuple(place)].set(low)
    longest = dims.index(max(dims))
    place[longest] = (place[longest] + 1) % dims[longest]
    return values.at[tuple(place)].set(high)


def level_of(stream_key, shape, shards, low, largest):
    level, own = 1.0, jax.random.fold_in(stream_key, 6)
    for position, blocks in shards:
        steps = jnp.exp(jax.random.uniform(jax.random.fold_in(own, position), (blocks,), jnp.float32, low / len(shards), largest / len(shards)))
        level = level * jnp.repeat(steps, shape[position] // blocks).reshape([-1 if axis == position else 1 for axis in range(len(shape))])
    return level


def centred(stream_key, dims, width, reach, pieces=(), held_as=jnp.bfloat16):
    gain = level_of(stream_key, dims, pieces, -0.22, 0.18) if pieces else 1.0
    result = jax.random.normal(stream_key, dims, jnp.float32) * width * gain
    return jnp.minimum(jnp.maximum(result, -reach), reach).astype(held_as)


def setup_inputs(seed: int = 0) -> dict:
    arg_keys = jax.random.split(jax.random.key(seed), 5)
    return {
        "u_panel": centred(arg_keys[0], (NT, K, NB), 1.0, 6.0, ((0, 32), (2, 8))),
        "v_panel": centred(arg_keys[1], (NT, K, NB), NB ** -0.5, 0.125, ((0, 32), (2, 8))),
        "ranks": place_ends(jax.random.randint(arg_keys[2], (NT,), K // 3, K + 1), jax.random.fold_in(arg_keys[2], 1), K // 3, K).astype(jnp.int32),
        "inverse_t": draw_inverse_t(jax.random.fold_in(arg_keys[4], 71), 0),
    }


def reference(u_panel, v_panel, ranks, inverse_t):
    within = jnp.arange(K, dtype=jnp.int32)[None, :, None] < ranks[:, None, None]
    masked = jnp.where(within, v_panel, jnp.zeros_like(v_panel))
    flat_rows = masked.astype(jnp.float32).reshape(NT * K, NB)
    panel_v = jnp.dot(flat_rows, inverse_t, precision=lax.Precision.HIGHEST,
                      preferred_element_type=jnp.float32).reshape(NT, K, NB).astype(jnp.bfloat16)
    slot_index = jnp.arange(JD, dtype=jnp.int32)
    group_index = jnp.arange(N_COL, dtype=jnp.int32)
    owner_tile = (group_index[:, None] + N_COL * (slot_index[None, :] // TPD)) * TPD + slot_index[None, :] % TPD
    columns = panel_v[owner_tile].astype(jnp.float32)

    def one_row(pair):
        row_factor, factor = pair
        core_blocks = jnp.einsum('kn,cqln->cqkl', row_factor.astype(jnp.float32), columns).astype(jnp.bfloat16)
        return jnp.einsum('cqkl,kn->cqln', core_blocks.astype(jnp.float32), factor.astype(jnp.float32)).astype(jnp.bfloat16)

    update_left = lax.map(one_row, (panel_v, u_panel))
    return panel_v, update_left
```

```python
import jax
import jax.numpy as jnp
from jax import lax
from jax.experimental import pallas as pl
from jax.experimental.pallas import tpu as pltpu
from jax.sharding import Mesh, PartitionSpec as P

AXES = ("z", "x", "y", "core")
SIZES = (8, 4, 4, 2)


def permute(value, target):
    pairs = []
    for z in range(8):
        for x in range(4):
            for y in range(4):
                for core in range(2):
                    goal = [p % s for p, s in zip(target(z, x, y, core), SIZES)]
                    source = ((z * 4 + x) * 4 + y) * 2 + core
                    pairs.append((source, ((goal[0] * 4 + goal[1]) * 4 + goal[2]) * 2 + goal[3]))
    return lax.ppermute(value, AXES, pairs)


def along_x(value, step):
    return permute(value, lambda z, x, y, core: (z, x + step, y, core))


def ring_of_four(value, shift, dim):
    below, above = shift(value, 1), shift(value, -1)
    half = value.shape[dim] // 2
    first = lax.slice_in_dim(below, 0, half, axis=dim)
    second = lax.slice_in_dim(above, half, value.shape[dim], axis=dim)
    across = jnp.concatenate([shift(first, 1), shift(second, -1)], axis=dim)
    return [value, above, across, below]


def along_y(value, step):
    return permute(value, lambda z, x, y, core: (z, x, y + step, core))


def along_z(value, step):
    return permute(value, lambda z, x, y, core: (z + step, x, y, core))


def ring_of_eight(value, shift):
    below, above, back = [value], [value], []
    for _ in range(3):
        below.append(shift(below[-1], 1))
        above.append(shift(above[-1], -1))
    half = value.shape[1] // 2
    first = shift(below[3][:, :half], 1)
    second = shift(above[3][:, half:], -1)
    across = jnp.concatenate([first, second], axis=1)
    return above + [across] + below[:0:-1]


def partial_kernel(place, *refs):
    rows, lines, kept, given = refs[:4], refs[4:12], refs[12], refs[13]
    kept[...] = jnp.zeros_like(kept)
    given[...] = jnp.zeros_like(given)
    z, core, mid = place[0], place[1], place[2]
    for far, line in enumerate(lines):
        at = lax.rem(z + far, 8)
        y = lax.rem(lax.div(at, 2) + 4 - mid, 4)
        mine = lax.rem(at, 2) == core
        column = jnp.concatenate([line[0], line[1]], axis=1)
        for step, row in enumerate(rows):
            block = jnp.concatenate([row[y, 0], row[y, 1]], axis=1)
            part = lax.dot_general(column, block, (((0,), (0,)), ((), ())), preferred_element_type=jnp.float32)

            @pl.when(mine)
            def _():
                kept[step] += part

            @pl.when(jnp.logical_not(mine))
            def _():
                given[step] += part


def partial_cores(rows, lines):
    place = jnp.stack([lax.axis_index(name) for name in ("z", "core", "y")]).astype(jnp.int32)
    wide = 2 * rows[0].shape[-1]
    vmem = pl.BlockSpec(memory_space=pltpu.VMEM)
    out = jax.ShapeDtypeStruct((4, wide, wide), jnp.float32)
    return pl.pallas_call(
        partial_kernel,
        out_shape=(out, out),
        in_specs=[pl.BlockSpec(memory_space=pltpu.SMEM)] + [vmem] * 12,
        out_specs=(vmem, vmem),
        compiler_params=pltpu.CompilerParams(vmem_limit_bytes=32 * 2**20),
        cost_estimate=pl.CostEstimate(flops=1400000000, bytes_accessed=6000000, transcendentals=0),
    )(place, *rows, *lines)


def apply_kernel(place, cores, left, out):
    step = pl.program_id(1)
    for tile in range(2):
        for column in range(2):
            block = cores[step, column * 128:(column + 1) * 128, tile * 128:(tile + 1) * 128]
            out[tile, 0, column] = lax.dot_general(
                block, left[tile], (((1,), (1,)), ((), ())), preferred_element_type=jnp.float32
            ).astype(out.dtype)


def apply_cores(cores, left):
    tiles, order, slots = left.shape
    place = lax.axis_index("x").astype(jnp.int32).reshape(1)
    parts = 2
    span = order // parts
    grid_spec = pltpu.PrefetchScalarGridSpec(
        num_scalar_prefetch=1,
        grid=(parts, 4),
        in_specs=[
            pl.BlockSpec(cores.shape, lambda n, step, place: (0, 0, 0)),
            pl.BlockSpec((tiles, span, slots), lambda n, step, place: (0, n, 0)),
        ],
        out_specs=pl.BlockSpec(
            (tiles, 1, 2, slots, span), lambda n, step, place: (0, 0, lax.rem(place[0] + 4 - step, 4), 0, n)
        ),
    )
    return pl.pallas_call(
        apply_kernel,
        out_shape=jax.ShapeDtypeStruct((tiles, 1, 8, slots, order), jnp.bfloat16),
        grid_spec=grid_spec,
        compiler_params=pltpu.CompilerParams(vmem_limit_bytes=32 * 2**20),
        cost_estimate=pl.CostEstimate(flops=1400000000, bytes_accessed=12000000, transcendentals=0),
    )(place, cores, left)


def local(u_panel, v_panel, ranks, inverse_t):
    tiles, slots, width = v_panel.shape
    x = lax.axis_index("x")
    within = lax.broadcasted_iota(jnp.int32, (1, 1, slots), 2) < ranks[:, None, None]
    own = jnp.swapaxes(v_panel, 1, 2)
    own = jnp.where(within, own, jnp.zeros_like(own))
    right = lax.all_gather(own, ("y", "core"), axis=1, tiled=True)
    left = lax.all_gather(jnp.swapaxes(u_panel, 1, 2), ("y", "core"), axis=1, tiled=True)

    depth = inverse_t.shape[0]
    rows = lax.broadcasted_iota(jnp.int32, inverse_t.shape, 0) + depth * (lax.axis_index("z") * 4 + x)
    cols = lax.broadcasted_iota(jnp.int32, inverse_t.shape, 1) + width * (lax.axis_index("y") * 2 + lax.axis_index("core"))
    nearest = lax.reduce_precision(inverse_t, 8, 7)
    rounded = nearest.astype(jnp.bfloat16)
    rest = jnp.where(rows == cols, inverse_t - nearest, 0.0)
    rest = jnp.sum(rest, axis=0, keepdims=True).astype(jnp.bfloat16)
    sent = jnp.concatenate([rounded, jnp.pad(rest, ((0, 15), (0, 0)))], axis=0)
    planes = lax.all_to_all(
        jnp.broadcast_to(sent[None], (8,) + sent.shape), "z", split_axis=0, concat_axis=0, tiled=True
    )
    blocks = ring_of_four(planes, along_x, 0)
    by_x = right.reshape(tiles, 8, 4, depth, slots)
    total = jnp.zeros((tiles, width, slots), jnp.float32)
    diagonal = jnp.zeros((width,), jnp.float32)
    for step, block in enumerate(blocks):
        part = lax.dynamic_index_in_dim(by_x, (x + step) % 4, axis=2, keepdims=False)
        total = total + jnp.einsum(
            "zmn,tzmk->tnk", block[:, :depth], part, preferred_element_type=jnp.float32
        )
        diagonal = diagonal + jnp.sum(block[:, depth].astype(jnp.float32), axis=0)
    total = total + diagonal[None, :, None] * own.astype(jnp.float32)
    solved = total.astype(jnp.bfloat16)

    moved = permute(
        solved,
        lambda z, x, y, core: (2 * y + x % 2, z // 2, 2 * (z % 2) + x // 2, core),
    )
    rows = ring_of_four(jnp.stack(ring_of_four(solved, along_y, 1)), along_x, 0)
    lines = ring_of_eight(moved, along_z)
    kept, given = partial_cores(rows, lines)
    given = permute(given, lambda z, x, y, core: (z, x, y, core + 1))
    cores = (kept + given).astype(jnp.bfloat16)
    pieces = [cores[0]] + [along_x(cores[step], step) for step in range(1, 4)]
    update = apply_cores(jnp.stack(pieces), left)
    return jnp.swapaxes(solved, 1, 2), update


def solution(mesh):
    fine = Mesh(mesh.devices.reshape(SIZES), AXES)
    row, col = ("z", "x"), ("y", "core")
    placed = (P(row, None, col), P(row, None, col), P(row), P(row, col))
    return jax.shard_map(
        local,
        mesh=fine,
        in_specs=placed,
        out_specs=(P(row, None, col), P(row, col, None, None, None)),
        check_vma=False,
    )
```

```python
import jax
import jax.numpy as jnp
from jax import lax
from jax.experimental import pallas as pl
from jax.experimental.pallas import tpu as pltpu
from jax.sharding import Mesh, PartitionSpec as P

AXES = ("z", "x", "y", "core")
SIZES = (8, 4, 4, 2)


def permute(value, target):
    pairs = []
    for z in range(8):
        for x in range(4):
            for y in range(4):
                for core in range(2):
                    goal = [p % s for p, s in zip(target(z, x, y, core), SIZES)]
                    source = ((z * 4 + x) * 4 + y) * 2 + core
                    pairs.append((source, ((goal[0] * 4 + goal[1]) * 4 + goal[2]) * 2 + goal[3]))
    return lax.ppermute(value, AXES, pairs)


def along_x(value, step):
    return permute(value, lambda z, x, y, core: (z, x + step, y, core))


def ring_of_four(value, shift, dim, after=None):
    below, above = shift(value, 1), shift(value, -1)
    if after is not None:
        below, above, after = lax.optimization_barrier((below, above, after))
    half = value.shape[dim] // 2
    first = lax.slice_in_dim(below, 0, half, axis=dim)
    second = lax.slice_in_dim(above, half, value.shape[dim], axis=dim)
    across = jnp.concatenate([shift(first, 1), shift(second, -1)], axis=dim)
    gathered = [value, above, across, below]
    return gathered if after is None else (gathered, after)


def along_y(value, step):
    return permute(value, lambda z, x, y, core: (z, x, y + step, core))


def along_z(value, step):
    return permute(value, lambda z, x, y, core: (z + step, x, y, core))


def ring_of_eight(value, shift, after):
    below, above = [value], [value]
    for step in range(3):
        near, far = shift(below[-1], 1), shift(above[-1], -1)
        if step == 0:
            near, far, after = lax.optimization_barrier((near, far, after))
        below.append(near)
        above.append(far)
    half = value.shape[1] // 2
    first = shift(below[3][:, :half], 1)
    second = shift(above[3][:, half:], -1)
    across = jnp.concatenate([first, second], axis=1)
    return above + [across] + below[:0:-1], after


def partial_kernel(place, *refs):
    rows, lines, kept, given, columns = refs[:4], refs[4:12], refs[12], refs[13], refs[14]
    first, core, mid = place[0], place[1], place[2]
    for far, line in enumerate(lines):
        at = lax.rem(first + far, 8)
        start = pl.multiple_of(320 * lax.rem(at, 4), 64)
        side = lax.rem(lax.div(at, 4) + core, 2)
        columns[side, pl.ds(start, 320), :] = jnp.concatenate([line[0], line[1]], axis=1)
    mine, others = columns[0].T, columns[1].T
    for step, row in enumerate(rows):
        near = [lax.rem(y + 4 - mid, 4) for y in range(4)]
        block = jnp.concatenate([jnp.concatenate([row[at, 0], row[at, 1]], axis=1) for at in near], axis=0)
        kept[step] = jnp.dot(mine, block, preferred_element_type=jnp.float32)
        given[step] = jnp.dot(others, block, preferred_element_type=jnp.float32)


def partial_cores(rows, lines):
    z, x, y, core = (lax.axis_index(name).astype(jnp.int32) for name in AXES)
    first = z - 2 * ((x - 2 * (y % 2) - 1) % 4) - y // 2 - 2
    place = jnp.stack([first % 8, core, y])
    wide = 2 * rows[0].shape[-1]
    vmem = pl.BlockSpec(memory_space=pltpu.VMEM)
    out = jax.ShapeDtypeStruct((4, wide, wide), jnp.float32)
    return pl.pallas_call(
        partial_kernel,
        out_shape=(out, out),
        in_specs=[pl.BlockSpec(memory_space=pltpu.SMEM)] + [vmem] * 12,
        out_specs=(vmem, vmem),
        scratch_shapes=[pltpu.VMEM((2, 1280, wide), rows[0].dtype)],
        compiler_params=pltpu.CompilerParams(vmem_limit_bytes=32 * 2**20),
        cost_estimate=pl.CostEstimate(flops=1400000000, bytes_accessed=6000000, transcendentals=0),
    )(place, *rows, *lines)


def apply_kernel(place, cores, left, *refs):
    out = refs[-1]
    for tile in range(2):
        product = jnp.dot(
            cores[:, tile * 128:(tile + 1) * 128], left[tile], preferred_element_type=jnp.float32
        ).astype(out.dtype)
        for column in range(2):
            out[tile, 0, column] = product[128 * column:128 * column + 128]


def apply_cores(step, cores, left, so_far=None):
    tiles, slots, order = left.shape
    _, x, y, core = (lax.axis_index(name).astype(jnp.int32) for name in AXES)
    place = ((x - 2 * (y % 2) - core - step) % 4).reshape(1)
    span = 1280
    earlier = [] if so_far is None else [so_far]
    grid_spec = pltpu.PrefetchScalarGridSpec(
        num_scalar_prefetch=1,
        grid=(order // span,),
        in_specs=[
            pl.BlockSpec(cores.shape, lambda n, place: (0, 0)),
            pl.BlockSpec((tiles, slots, span), lambda n, place: (0, 0, n)),
        ] + [pl.BlockSpec(memory_space=pl.ANY)] * len(earlier),
        out_specs=pl.BlockSpec((tiles, 1, 2, slots, span), lambda n, place: (0, 0, place[0], 0, n)),
    )
    return pl.pallas_call(
        apply_kernel,
        out_shape=jax.ShapeDtypeStruct((tiles, 1, 8, slots, order), jnp.bfloat16),
        grid_spec=grid_spec,
        input_output_aliases={3: 0} if earlier else {},
        compiler_params=pltpu.CompilerParams(vmem_limit_bytes=32 * 2**20),
        cost_estimate=pl.CostEstimate(flops=350000000, bytes_accessed=4000000, transcendentals=0),
    )(place, cores, left, *earlier)


VMEM = pl.BlockSpec(memory_space=pltpu.VMEM)
SMEM = pl.BlockSpec(memory_space=pltpu.SMEM)


def local_call(kernel, shapes, *operands, flops=0, bytes_accessed=4000000):
    outs = [jax.ShapeDtypeStruct(shape, dtype) for shape, dtype in shapes]
    return pl.pallas_call(
        kernel,
        out_shape=outs,
        in_specs=[SMEM] + [VMEM] * (len(operands) - 1),
        out_specs=[VMEM] * len(outs),
        compiler_params=pltpu.CompilerParams(vmem_limit_bytes=32 * 2**20),
        cost_estimate=pl.CostEstimate(flops=flops, bytes_accessed=bytes_accessed, transcendentals=0),
    )(*operands)


def pack_kernel(place, inverse, out):
    exact = inverse[...]
    rounded = exact.astype(jnp.bfloat16).astype(jnp.float32)
    rows = lax.broadcasted_iota(jnp.int32, exact.shape, 0) + place[0]
    cols = lax.broadcasted_iota(jnp.int32, exact.shape, 1) + place[1]
    rest = jnp.sum(jnp.where(rows == cols, exact - rounded, 0.0), axis=0, keepdims=True)
    tail = jnp.concatenate([rounded[48:, 256:], jnp.zeros((16, 64), jnp.float32)], axis=0)
    ends = jnp.concatenate([rounded[:48, 256:], tail], axis=1)
    last = jnp.concatenate([rest[:, 256:], jnp.zeros((1, 64), jnp.float32)], axis=1)
    rest = jnp.concatenate([rest[:, :128], rest[:, 128:256], last, jnp.zeros((13, 128), jnp.float32)], axis=0)
    packed = jnp.concatenate([rounded[:, :128], rounded[:, 128:256], ends, rest], axis=0).astype(jnp.bfloat16)
    for copy in range(8):
        out[copy] = packed


def arrange_kernel(place, own, other, full, mine):
    x, mid = place[0], place[1]
    for step in range(4):
        start = pl.multiple_of(80 * lax.rem(x + step, 4), 16)
        low, high = [], []
        for side in (own, other):
            for y in range(4):
                near = lax.rem(y + 4 - mid, 4)
                part = jnp.concatenate([side[near, 2 + tile, pl.ds(start, 80), :] for tile in range(2)], axis=1)
                low.append(part[:48])
                high.append(part[48:])
        full[step] = jnp.concatenate(low + high, axis=0).T
    here = jnp.concatenate([own[0, 2], own[0, 3]], axis=1)
    mine[...] = jnp.concatenate([here, jnp.zeros((64, 256), here.dtype)], axis=0).T


def left_kernel(place, own, other, left, rows):
    mid, core = place[1], place[2]
    for tile in range(2):
        for side, at in ((own, core), (other, 1 - core)):
            for near in range(4):
                y = lax.rem(mid + near, 4)
                rows[pl.ds(pl.multiple_of(640 * y + 320 * at, 64), 320), :] = side[near, tile]
        left[tile] = rows[...].T


def solve_kernel(place, full, mine, *refs):
    blocks, out = refs[:4], refs[4]
    core = place[2]
    order = [2 * y + core for y in range(4)] + [2 * y + 1 - core for y in range(4)]
    wide = jnp.zeros((256, 256), jnp.float32)
    first = jnp.zeros((256, 128), jnp.float32)
    second = jnp.zeros((256, 128), jnp.float32)
    rest = jnp.zeros((16, 128), jnp.float32)
    for step, block in enumerate(blocks):
        parts = [
            jnp.concatenate(
                [block[at, low:low + 48, :] for at in order] + [block[at, low + 48:low + 80, :] for at in order], axis=0
            )
            for low in (0, 80)
        ]
        ends = jnp.concatenate([block[at, 160:208, :] for at in order], axis=0)
        tails = jnp.concatenate([block[at, 160:192, :] for at in order], axis=0)
        rows = full[step]
        wide += jnp.dot(rows, jnp.concatenate(parts, axis=1), preferred_element_type=jnp.float32)
        first += jnp.dot(rows[:, :384], ends, preferred_element_type=jnp.float32)
        second += jnp.dot(rows[:, 384:], tails, preferred_element_type=jnp.float32)
        for at in range(8):
            rest += block[at, 208:224, :].astype(jnp.float32)
    own = mine[...].astype(jnp.float32)
    wide += own[:, :256] * jnp.concatenate([rest[0:1], rest[1:2]], axis=1)
    first += own[:, 256:] * rest[2:3]
    ends = first.T[:64] + second.T[64:]
    total = jnp.concatenate([wide.T, ends], axis=0)
    slot = lax.broadcasted_iota(jnp.int32, (320, 128), 1)
    for tile in range(2):
        part = total[:, tile * 128:(tile + 1) * 128]
        out[tile] = jnp.where(slot < place[3 + tile], part, 0.0).astype(out.dtype)


def local(u_panel, v_panel, ranks, inverse_t):
    tiles, slots, width = v_panel.shape
    depth = inverse_t.shape[0]
    z, x, y, core = (lax.axis_index(name).astype(jnp.int32) for name in AXES)
    place = jnp.stack([x, y, core, ranks[0], ranks[1], z])
    corner = jnp.stack([depth * (z * 4 + x), width * (y * 2 + core)])
    half = jnp.bfloat16

    (sent,) = local_call(pack_kernel, [((8, 224, 128), half)], corner, inverse_t)
    both = jnp.concatenate([jnp.swapaxes(u_panel, 1, 2), jnp.swapaxes(v_panel, 1, 2)], axis=0)
    both, sent = lax.optimization_barrier((both, sent))
    planes = lax.all_to_all(sent, "z", split_axis=0, concat_axis=0, tiled=True)
    own, planes = ring_of_four(both, along_y, 1, after=planes)
    own = jnp.stack(own)
    blocks, own = ring_of_four(planes, along_x, 0, after=own)
    other = permute(own, lambda z, x, y, core: (z, x, y, core + 1))
    full, mine = local_call(arrange_kernel, [((4, 256, 640), half), ((256, 384), half)], place, own, other)
    left = pl.pallas_call(
        left_kernel,
        out_shape=jax.ShapeDtypeStruct((tiles, slots, 8 * width), half),
        in_specs=[SMEM, VMEM, VMEM],
        out_specs=VMEM,
        scratch_shapes=[pltpu.VMEM((8 * width, slots), half)],
        compiler_params=pltpu.CompilerParams(vmem_limit_bytes=32 * 2**20),
        cost_estimate=pl.CostEstimate(flops=0, bytes_accessed=4000000, transcendentals=0),
    )(place, own, other)
    (solved,) = local_call(
        solve_kernel, [((tiles, width, slots), half)], place, full, mine, *blocks, flops=500000000
    )

    moved = permute(
        solved,
        lambda z, x, y, core: (
            z + y - 2 * (x % 2),
            x + z // 2,
            2 * (z % 2) + x // 2,
            core,
        ),
    )
    rows, moved = ring_of_four(solved, along_y, 1, after=moved)
    rows = jnp.stack(rows)
    lines, rows = ring_of_eight(moved, along_z, rows)
    rows = ring_of_four(rows, along_x, 0)
    kept, given = partial_cores(rows, lines)
    given = permute(given, lambda z, x, y, core: (z, x, y, core + 1))
    cores = (kept + given).astype(half)
    pieces = [cores[0]] + [along_x(cores[step], step) for step in range(1, 4)]
    update = apply_cores(0, pieces[0], left)
    for step in (1, 3, 2):
        update = apply_cores(step, pieces[step], left, update)
    return jnp.swapaxes(solved, 1, 2), update


def solution(mesh):
    fine = Mesh(mesh.devices.reshape(SIZES), AXES)
    row, col = ("z", "x"), ("y", "core")
    placed = (P(row, None, col), P(row, None, col), P(row), P(row, col))
    return jax.shard_map(
        local,
        mesh=fine,
        in_specs=placed,
        out_specs=(P(row, None, col), P(row, col, None, None, None)),
        check_vma=False,
    )
```

```python
import functools

import jax
import jax.numpy as jnp
from jax import lax
from jax.experimental import pallas as pl
from jax.experimental.pallas import tpu as pltpu
from jax.sharding import Mesh, PartitionSpec as P

AXES = ("z", "x", "y", "core")
SIZES = (8, 4, 4, 2)


def permute(value, target):
    pairs = []
    for z in range(8):
        for x in range(4):
            for y in range(4):
                for core in range(2):
                    goal = [p % s for p, s in zip(target(z, x, y, core), SIZES)]
                    source = ((z * 4 + x) * 4 + y) * 2 + core
                    pairs.append((source, ((goal[0] * 4 + goal[1]) * 4 + goal[2]) * 2 + goal[3]))
    return lax.ppermute(value, AXES, pairs)


def along_x(value, step):
    return permute(value, lambda z, x, y, core: (z, x + step, y, core))


def ring_of_four(value, shift, dim, after=None):
    below, above = shift(value, 1), shift(value, -1)
    if after is not None:
        below, above, after = lax.optimization_barrier((below, above, after))
    half = value.shape[dim] // 2
    first = lax.slice_in_dim(below, 0, half, axis=dim)
    second = lax.slice_in_dim(above, half, value.shape[dim], axis=dim)
    gathered = [value, above, (shift(first, 1), shift(second, -1)), below]
    return gathered if after is None else (gathered, after)


def flat(blocks):
    return jax.tree.leaves(blocks)


def stacked(blocks, dim):
    return jnp.stack([jnp.concatenate(b, axis=dim) if isinstance(b, tuple) else b for b in blocks])


def along_y(value, step):
    return permute(value, lambda z, x, y, core: (z, x, y + step, core))


def gather_y(value):
    far, above, below = along_y(value, 2), along_y(value, -1), along_y(value, 1)
    return jnp.stack([value, above, far, below])


def along_z(value, step):
    return permute(value, lambda z, x, y, core: (z + step, x, y, core))


def ring_of_eight(value, shift, after):
    below, above = [value], [value]
    for step in range(3):
        near, far = shift(below[-1], 1), shift(above[-1], -1)
        below.append(near)
        above.append(far)
    half = value.shape[1] // 2
    first = shift(below[3][:, :half], 1)
    second = shift(above[3][:, half:], -1)
    across = jnp.concatenate([first, second], axis=1)
    return above + [across] + below[:0:-1], after


def partial_kernel(place, *refs):
    rows, lines, (kept, given, columns) = refs[:4], refs[4:12], refs[12:]
    first, core, mid = place[0], place[1], place[2]
    for far, line in enumerate(lines):
        at = lax.rem(first + far, 8)
        start = pl.multiple_of(320 * lax.rem(at, 4), 64)
        side = lax.rem(lax.div(at, 4) + core, 2)
        columns[side, pl.ds(start, 320), :] = jnp.concatenate([line[0], line[1]], axis=1)
    mine, others = columns[0].T, columns[1].T
    for step, row in enumerate(rows):
        near = [lax.rem(y + 4 - mid, 4) for y in range(4)]
        block = jnp.concatenate([jnp.concatenate([row[at, 0], row[at, 1]], axis=1) for at in near], axis=0)
        kept[step] = jnp.dot(mine, block, preferred_element_type=jnp.float32)
        given[step] = jnp.dot(others, block, preferred_element_type=jnp.float32).astype(given.dtype)


def partial_cores(rows, lines):
    rows = [jnp.concatenate(row, axis=0) if isinstance(row, tuple) else row for row in rows]
    z, x, y, core = (lax.axis_index(name).astype(jnp.int32) for name in AXES)
    first = z - 2 * ((x - 2 * (y % 2) - 2) % 4) - y // 2 - 2
    place = jnp.stack([first % 8, core, y])
    wide = 2 * rows[0].shape[-1]
    vmem = pl.BlockSpec(memory_space=pltpu.VMEM)
    return pl.pallas_call(
        partial_kernel,
        out_shape=[jax.ShapeDtypeStruct((4, wide, wide), dtype) for dtype in (jnp.float32, jnp.float32)],
        in_specs=[pl.BlockSpec(memory_space=pltpu.SMEM)] + [vmem] * 12,
        out_specs=(vmem, vmem),
        scratch_shapes=[pltpu.VMEM((2, 1280, wide), rows[0].dtype)],
        compiler_params=pltpu.CompilerParams(vmem_limit_bytes=32 * 2**20),
        cost_estimate=pl.CostEstimate(flops=1400000000, bytes_accessed=6000000, transcendentals=0),
    )(place, *rows, *lines)


def apply_kernel(count, place, left, *refs):
    pieces = refs[:count]
    out, product, sems = refs[-3:]
    copies = []
    for number, cores in enumerate(pieces):
        for part in range(5):
            span = pl.ds(512 * part, 512)
            for tile in range(2):
                block = jnp.dot(
                    cores[:, tile * 128:(tile + 1) * 128], left[tile, :, span], preferred_element_type=jnp.float32
                ).astype(out.dtype)
                for column in range(2):
                    product[number, tile, column, :, span] = block[128 * column:128 * column + 128]
                copies.append(
                    pltpu.make_async_copy(
                        product.at[number, tile, :, :, span],
                        out.at[tile, 0, pl.ds(2 * place[number], 2), :, span],
                        sems.at[number, part, tile],
                    )
                )
                copies[-1].start()
    for copy in copies:
        copy.wait()


def apply_cores(steps, pieces, left, so_far=None):
    tiles, slots, order = left.shape
    _, x, y, core = (lax.axis_index(name).astype(jnp.int32) for name in AXES)
    place = jnp.stack([(x - 2 * (y % 2) - 2 * core - step) % 4 for step in steps])
    count = len(steps)
    earlier = [] if so_far is None else [so_far]
    return pl.pallas_call(
        functools.partial(apply_kernel, count),
        out_shape=jax.ShapeDtypeStruct((tiles, 1, 8, slots, order), jnp.bfloat16),
        in_specs=[SMEM] + [VMEM] * (1 + count) + [pl.BlockSpec(memory_space=pl.ANY)] * len(earlier),
        out_specs=pl.BlockSpec(memory_space=pl.ANY),
        input_output_aliases={2 + count: 0} if earlier else {},
        scratch_shapes=[pltpu.VMEM((count, tiles, 2, slots, order), jnp.bfloat16), pltpu.SemaphoreType.DMA((count, 5, 2))],
        compiler_params=pltpu.CompilerParams(vmem_limit_bytes=32 * 2**20),
        cost_estimate=pl.CostEstimate(flops=350000000 * count, bytes_accessed=4000000 * count, transcendentals=0),
    )(place, left, *pieces, *earlier)


VMEM = pl.BlockSpec(memory_space=pltpu.VMEM)
SMEM = pl.BlockSpec(memory_space=pltpu.SMEM)


def local_call(kernel, shapes, *operands, flops=0, bytes_accessed=4000000):
    outs = [jax.ShapeDtypeStruct(shape, dtype) for shape, dtype in shapes]
    return pl.pallas_call(
        kernel,
        out_shape=outs,
        in_specs=[SMEM] + [VMEM] * (len(operands) - 1),
        out_specs=[VMEM] * len(outs),
        compiler_params=pltpu.CompilerParams(vmem_limit_bytes=32 * 2**20),
        cost_estimate=pl.CostEstimate(flops=flops, bytes_accessed=bytes_accessed, transcendentals=0),
    )(*operands)


def pack_kernel(place, inverse, out):
    exact = inverse[...]
    rounded = exact.astype(jnp.bfloat16).astype(jnp.float32)
    rows = lax.broadcasted_iota(jnp.int32, exact.shape, 0) + place[0]
    cols = lax.broadcasted_iota(jnp.int32, exact.shape, 1) + place[1]
    rest = jnp.sum(jnp.where(rows == cols, exact - rounded, 0.0), axis=0, keepdims=True)
    rests = [rest[:, at:at + 64] for at in range(0, 320, 64)]
    tail = jnp.concatenate([rounded[48:, 256:]] + rests + [jnp.zeros((11, 64), jnp.float32)], axis=0)
    ends = jnp.concatenate([rounded[:48, 256:], tail], axis=1)
    packed = jnp.concatenate([rounded[:, :128], rounded[:, 128:256], ends], axis=0).astype(jnp.bfloat16)
    for copy in range(8):
        out[copy] = packed


def arrange_kernel(place, own, other, full, mine):
    x, mid = place[0], place[1]
    for step in range(4):
        start = pl.multiple_of(80 * lax.rem(x + step, 4), 16)
        low, high = [], []
        for side in (own, other):
            for y in range(4):
                near = lax.rem(y + 4 - mid, 4)
                part = jnp.concatenate([side[near, 2 + tile, pl.ds(start, 80), :] for tile in range(2)], axis=1)
                low.append(part[:48])
                high.append(part[48:])
        full[step] = jnp.concatenate(low + high, axis=0).T
    here = jnp.concatenate([own[0, 2], own[0, 3]], axis=1)
    mine[...] = jnp.concatenate([here, jnp.zeros((64, 256), here.dtype)], axis=0).T


def left_kernel(place, own, other, left, rows):
    mid, core = place[1], place[2]
    for tile in range(2):
        for side, at in ((own, core), (other, 1 - core)):
            for near in range(4):
                y = lax.rem(mid + near, 4)
                rows[pl.ds(pl.multiple_of(640 * y + 320 * at, 64), 320), :] = side[near, tile]
        left[tile] = rows[...].T


def solve_kernel(place, full, mine, here, above, first, second, below, out):
    core = place[2]
    order = [2 * y + core for y in range(4)] + [2 * y + 1 - core for y in range(4)]
    wide = jnp.zeros((256, 256), jnp.float32)
    lows = jnp.zeros((256, 128), jnp.float32)
    highs = jnp.zeros((256, 128), jnp.float32)
    rest = jnp.zeros((16, 128), jnp.float32)
    for step in range(4):
        if step == 2:
            blocks = [(first if at % 4 < 2 else second, order[at] - at % 4 // 2 * 4) for at in range(8)]
        else:
            blocks = [((here, above, None, below)[step], at) for at in order]
        parts = [
            jnp.concatenate(
                [ref[at, low:low + 48, :] for ref, at in blocks] + [ref[at, low + 48:low + 80, :] for ref, at in blocks],
                axis=0,
            )
            for low in (0, 80)
        ]
        ends = jnp.concatenate([ref[at, 160:208, :] for ref, at in blocks], axis=0)
        tails = jnp.concatenate([ref[at, 160:192, :] for ref, at in blocks], axis=0)
        rows = full[step]
        wide += jnp.dot(rows, jnp.concatenate(parts, axis=1), preferred_element_type=jnp.float32)
        lows += jnp.dot(rows[:, :384], ends, preferred_element_type=jnp.float32)
        highs += jnp.dot(rows[:, 384:], tails, preferred_element_type=jnp.float32)
        for ref, at in blocks:
            rest += ref[at, 192:208, :].astype(jnp.float32)
    own = mine[...].astype(jnp.float32)
    rest = rest[:, 64:]
    wide += own[:, :256] * jnp.concatenate([rest[at:at + 1] for at in range(4)], axis=1)
    lows += own[:, 256:] * jnp.concatenate([rest[4:5], jnp.zeros((1, 64), jnp.float32)], axis=1)
    ends = lows.T[:64] + highs.T[64:]
    total = jnp.concatenate([wide.T, ends], axis=0)
    slot = lax.broadcasted_iota(jnp.int32, (320, 128), 1)
    for tile in range(2):
        part = total[:, tile * 128:(tile + 1) * 128]
        out[tile] = jnp.where(slot < place[3 + tile], part, 0.0).astype(out.dtype)


def local(u_panel, v_panel, ranks, inverse_t):
    tiles, slots, width = v_panel.shape
    depth = inverse_t.shape[0]
    z, x, y, core = (lax.axis_index(name).astype(jnp.int32) for name in AXES)
    place = jnp.stack([x, y, core, ranks[0], ranks[1], z])
    corner = jnp.stack([depth * (z * 4 + x), width * (y * 2 + core)])
    half = jnp.bfloat16

    (sent,) = local_call(pack_kernel, [((8, 208, 128), half)], corner, inverse_t)
    both = jnp.concatenate([jnp.swapaxes(u_panel, 1, 2), jnp.swapaxes(v_panel, 1, 2)], axis=0)
    both, sent = lax.optimization_barrier((both, sent))
    planes = lax.all_to_all(sent, "z", split_axis=0, concat_axis=0, tiled=True)
    own = gather_y(both)
    blocks, own = ring_of_four(planes, along_x, 0, after=own)
    other = permute(own, lambda z, x, y, core: (z, x, y, core + 1))
    full, mine = local_call(arrange_kernel, [((4, 256, 640), half), ((256, 384), half)], place, own, other)
    left = pl.pallas_call(
        left_kernel,
        out_shape=jax.ShapeDtypeStruct((tiles, slots, 8 * width), half),
        in_specs=[SMEM, VMEM, VMEM],
        out_specs=VMEM,
        scratch_shapes=[pltpu.VMEM((8 * width, slots), half)],
        compiler_params=pltpu.CompilerParams(vmem_limit_bytes=32 * 2**20),
        cost_estimate=pl.CostEstimate(flops=0, bytes_accessed=4000000, transcendentals=0),
    )(place, own, other)
    (solved,) = local_call(
        solve_kernel, [((tiles, width, slots), half)], place, full, mine, *flat(blocks), flops=500000000
    )

    moved = permute(
        solved,
        lambda z, x, y, core: (
            z + y - 2,
            x + z // 2 + x % 2,
            2 * (z % 2) + x // 2,
            core,
        ),
    )
    rows, moved = lax.optimization_barrier((gather_y(solved), moved))
    lines, rows = ring_of_eight(moved, along_z, rows)
    rows = ring_of_four(rows, along_x, 0)
    kept, given = partial_cores(rows, lines)
    given = permute(given, lambda z, x, y, core: (z, x, y, core + 1))
    cores = (kept + given.astype(jnp.float32)).astype(half)
    pieces = [cores[0]] + [along_x(cores[step], step) for step in (1, 2, 3)]
    update = apply_cores([0], [pieces[0]], left)
    for step in (1, 3, 2):
        update = apply_cores([step], [pieces[step]], left, update)
    return jnp.swapaxes(solved, 1, 2), update


def solution(mesh):
    fine = Mesh(mesh.devices.reshape(SIZES), AXES)
    row, col = ("z", "x"), ("y", "core")
    placed = (P(row, None, col), P(row, None, col), P(row), P(row, col))
    return jax.shard_map(
        local,
        mesh=fine,
        in_specs=placed,
        out_specs=(P(row, None, col), P(row, col, None, None, None)),
        check_vma=False,
    )
```

```python
import functools

import jax
import jax.numpy as jnp
from jax import lax
from jax.experimental import pallas as pl
from jax.experimental.pallas import tpu as pltpu
from jax.sharding import Mesh, PartitionSpec as P

AXES = ("z", "x", "y", "core")
SIZES = (8, 4, 4, 2)


def permute(value, target):
    pairs = []
    for z in range(8):
        for x in range(4):
            for y in range(4):
                for core in range(2):
                    goal = [p % s for p, s in zip(target(z, x, y, core), SIZES)]
                    source = ((z * 4 + x) * 4 + y) * 2 + core
                    pairs.append((source, ((goal[0] * 4 + goal[1]) * 4 + goal[2]) * 2 + goal[3]))
    return lax.ppermute(value, AXES, pairs)


def along_x(value, step):
    return permute(value, lambda z, x, y, core: (z, x + step, y, core))


def ring_of_four(value, shift, dim, after=None):
    below, above = shift(value, 1), shift(value, -1)
    if after is not None:
        below, above, after = lax.optimization_barrier((below, above, after))
    half = value.shape[dim] // 2
    first = lax.slice_in_dim(below, 0, half, axis=dim)
    second = lax.slice_in_dim(above, half, value.shape[dim], axis=dim)
    gathered = [value, above, (shift(first, 1), shift(second, -1)), below]
    return gathered if after is None else (gathered, after)


def flat(blocks):
    return jax.tree.leaves(blocks)


def stacked(blocks, dim):
    return jnp.stack([jnp.concatenate(b, axis=dim) if isinstance(b, tuple) else b for b in blocks])


def along_y(value, step):
    return permute(value, lambda z, x, y, core: (z, x, y + step, core))


def gather_y(value):
    far, above, below = along_y(value, 2), along_y(value, -1), along_y(value, 1)
    return jnp.stack([value, above, far, below])


def along_z(value, step):
    return permute(value, lambda z, x, y, core: (z + step, x, y, core))


def ring_of_eight(value, shift, after):
    below, above = [value], [value]
    for step in range(3):
        near, far = shift(below[-1], 1), shift(above[-1], -1)
        below.append(near)
        above.append(far)
    half = value.shape[1] // 2
    first = shift(below[3][:, :half], 1)
    second = shift(above[3][:, half:], -1)
    across = jnp.concatenate([first, second], axis=1)
    return above + [across] + below[:0:-1], after


def partial_kernel(place, *refs):
    rows, lines, (kept, given, columns) = refs[:4], refs[4:12], refs[12:]
    first, core, mid = place[0], place[1], place[2]
    for far, line in enumerate(lines):
        at = lax.rem(first + far, 8)
        start = pl.multiple_of(320 * lax.rem(at, 4), 64)
        side = lax.rem(lax.div(at, 4) + core, 2)
        columns[side, pl.ds(start, 320), :] = jnp.concatenate([line[0], line[1]], axis=1)
    mine, others = columns[0].T, columns[1].T
    for step, row in enumerate(rows):
        near = [lax.rem(y + 4 - mid, 4) for y in range(4)]
        block = jnp.concatenate([jnp.concatenate([row[at, 0], row[at, 1]], axis=1) for at in near], axis=0)
        kept[step] = jnp.dot(mine, block, preferred_element_type=jnp.float32)
        given[step] = jnp.dot(others, block, preferred_element_type=jnp.float32).astype(given.dtype)


def partial_cores(rows, lines):
    rows = [jnp.concatenate(row, axis=0) if isinstance(row, tuple) else row for row in rows]
    z, x, y, core = (lax.axis_index(name).astype(jnp.int32) for name in AXES)
    first = z - 2 * ((x - 2 * (y % 2) - 2) % 4) - y // 2 - 2
    place = jnp.stack([first % 8, core, y])
    wide = 2 * rows[0].shape[-1]
    vmem = pl.BlockSpec(memory_space=pltpu.VMEM)
    return pl.pallas_call(
        partial_kernel,
        out_shape=[jax.ShapeDtypeStruct((4, wide, wide), dtype) for dtype in (jnp.float32, jnp.float32)],
        in_specs=[pl.BlockSpec(memory_space=pltpu.SMEM)] + [vmem] * 12,
        out_specs=(vmem, vmem),
        scratch_shapes=[pltpu.VMEM((2, 1280, wide), rows[0].dtype)],
        compiler_params=pltpu.CompilerParams(vmem_limit_bytes=32 * 2**20),
        cost_estimate=pl.CostEstimate(flops=1400000000, bytes_accessed=6000000, transcendentals=0),
    )(place, *rows, *lines)


def apply_kernel(count, place, left, *refs):
    pieces = refs[:count]
    out, product, sems = refs[-3:]
    copies = []
    for number, cores in enumerate(pieces):
        for part in range(5):
            span = pl.ds(512 * part, 512)
            for tile in range(2):
                block = jnp.dot(
                    cores[:, tile * 128:(tile + 1) * 128], left[tile, :, span], preferred_element_type=jnp.float32
                ).astype(out.dtype)
                for column in range(2):
                    product[number, tile, column, :, span] = block[128 * column:128 * column + 128]
                copies.append(
                    pltpu.make_async_copy(
                        product.at[number, tile, :, :, span],
                        out.at[tile, 0, pl.ds(2 * place[number], 2), :, span],
                        sems.at[number, part, tile],
                    )
                )
                copies[-1].start()
    for copy in copies:
        copy.wait()


def apply_cores(steps, pieces, left, so_far=None):
    tiles, slots, order = left.shape
    _, x, y, core = (lax.axis_index(name).astype(jnp.int32) for name in AXES)
    place = jnp.stack([(x - 2 * (y % 2) - 2 * core - step) % 4 for step in steps])
    count = len(steps)
    earlier = [] if so_far is None else [so_far]
    return pl.pallas_call(
        functools.partial(apply_kernel, count),
        out_shape=jax.ShapeDtypeStruct((tiles, 1, 8, slots, order), jnp.bfloat16),
        in_specs=[SMEM] + [VMEM] * (1 + count) + [pl.BlockSpec(memory_space=pl.ANY)] * len(earlier),
        out_specs=pl.BlockSpec(memory_space=pl.ANY),
        input_output_aliases={2 + count: 0} if earlier else {},
        scratch_shapes=[pltpu.VMEM((count, tiles, 2, slots, order), jnp.bfloat16), pltpu.SemaphoreType.DMA((count, 5, 2))],
        compiler_params=pltpu.CompilerParams(vmem_limit_bytes=32 * 2**20),
        cost_estimate=pl.CostEstimate(flops=350000000 * count, bytes_accessed=4000000 * count, transcendentals=0),
    )(place, left, *pieces, *earlier)


VMEM = pl.BlockSpec(memory_space=pltpu.VMEM)
SMEM = pl.BlockSpec(memory_space=pltpu.SMEM)


def local_call(kernel, shapes, *operands, flops=0, bytes_accessed=4000000):
    outs = [jax.ShapeDtypeStruct(shape, dtype) for shape, dtype in shapes]
    return pl.pallas_call(
        kernel,
        out_shape=outs,
        in_specs=[SMEM] + [VMEM] * (len(operands) - 1),
        out_specs=[VMEM] * len(outs),
        compiler_params=pltpu.CompilerParams(vmem_limit_bytes=32 * 2**20),
        cost_estimate=pl.CostEstimate(flops=flops, bytes_accessed=bytes_accessed, transcendentals=0),
    )(*operands)


def pack_kernel(place, inverse, out):
    exact = inverse[...]
    rounded = exact.astype(jnp.bfloat16).astype(jnp.float32)
    rows = lax.broadcasted_iota(jnp.int32, exact.shape, 0) + place[0]
    cols = lax.broadcasted_iota(jnp.int32, exact.shape, 1) + place[1]
    rest = jnp.sum(jnp.where(rows == cols, exact - rounded, 0.0), axis=0, keepdims=True)
    rests = [rest[:, at:at + 64] for at in range(0, 320, 64)]
    tail = jnp.concatenate([rounded[48:, 256:]] + rests + [jnp.zeros((11, 64), jnp.float32)], axis=0)
    ends = jnp.concatenate([rounded[:48, 256:], tail], axis=1)
    packed = jnp.concatenate([rounded[:, :128], rounded[:, 128:256], ends], axis=0).astype(jnp.bfloat16)
    for copy in range(8):
        out[copy] = packed


def arrange_kernel(place, own, other, full, mine):
    x, mid = place[0], place[1]
    for step in range(4):
        start = pl.multiple_of(80 * lax.rem(x + step, 4), 16)
        low, high = [], []
        for side in (own, other):
            for y in range(4):
                near = lax.rem(y + 4 - mid, 4)
                part = jnp.concatenate([side[near, 2 + tile, pl.ds(start, 80), :] for tile in range(2)], axis=1)
                low.append(part[:48])
                high.append(part[48:])
        full[step] = jnp.concatenate(low + high, axis=0).T
    here = jnp.concatenate([own[0, 2], own[0, 3]], axis=1)
    mine[...] = jnp.concatenate([here, jnp.zeros((64, 256), here.dtype)], axis=0).T


def left_kernel(place, own, other, left, rows):
    mid, core = place[1], place[2]
    for tile in range(2):
        for side, at in ((own, core), (other, 1 - core)):
            for near in range(4):
                y = lax.rem(mid + near, 4)
                rows[pl.ds(pl.multiple_of(640 * y + 320 * at, 64), 320), :] = side[near, tile]
        left[tile] = rows[...].T


def solve_kernel(place, full, mine, here, above, first, second, below, out):
    core = place[2]
    order = [2 * y + core for y in range(4)] + [2 * y + 1 - core for y in range(4)]
    wide = jnp.zeros((256, 256), jnp.float32)
    lows = jnp.zeros((256, 128), jnp.float32)
    highs = jnp.zeros((256, 128), jnp.float32)
    rest = jnp.zeros((16, 128), jnp.float32)
    for step in range(4):
        if step == 2:
            blocks = [(first if at % 4 < 2 else second, order[at] - at % 4 // 2 * 4) for at in range(8)]
        else:
            blocks = [((here, above, None, below)[step], at) for at in order]
        parts = [
            jnp.concatenate(
                [ref[at, low:low + 48, :] for ref, at in blocks] + [ref[at, low + 48:low + 80, :] for ref, at in blocks],
                axis=0,
            )
            for low in (0, 80)
        ]
        ends = jnp.concatenate([ref[at, 160:208, :] for ref, at in blocks], axis=0)
        tails = jnp.concatenate([ref[at, 160:192, :] for ref, at in blocks], axis=0)
        rows = full[step]
        wide += jnp.dot(rows, jnp.concatenate(parts, axis=1), preferred_element_type=jnp.float32)
        lows += jnp.dot(rows[:, :384], ends, preferred_element_type=jnp.float32)
        highs += jnp.dot(rows[:, 384:], tails, preferred_element_type=jnp.float32)
        for ref, at in blocks:
            rest += ref[at, 192:208, :].astype(jnp.float32)
    own = mine[...].astype(jnp.float32)
    rest = rest[:, 64:]
    wide += own[:, :256] * jnp.concatenate([rest[at:at + 1] for at in range(4)], axis=1)
    lows += own[:, 256:] * jnp.concatenate([rest[4:5], jnp.zeros((1, 64), jnp.float32)], axis=1)
    ends = lows.T[:64] + highs.T[64:]
    total = jnp.concatenate([wide.T, ends], axis=0)
    slot = lax.broadcasted_iota(jnp.int32, (320, 128), 1)
    for tile in range(2):
        part = total[:, tile * 128:(tile + 1) * 128]
        out[tile] = jnp.where(slot < place[3 + tile], part, 0.0).astype(out.dtype)


def local(u_panel, v_panel, ranks, inverse_t):
    tiles, slots, width = v_panel.shape
    depth = inverse_t.shape[0]
    z, x, y, core = (lax.axis_index(name).astype(jnp.int32) for name in AXES)
    place = jnp.stack([x, y, core, ranks[0], ranks[1], z])
    corner = jnp.stack([depth * (z * 4 + x), width * (y * 2 + core)])
    half = jnp.bfloat16

    (sent,) = local_call(pack_kernel, [((8, 208, 128), half)], corner, inverse_t)
    both = jnp.concatenate([jnp.swapaxes(u_panel, 1, 2), jnp.swapaxes(v_panel, 1, 2)], axis=0)
    both, sent = lax.optimization_barrier((both, sent))
    planes = lax.all_to_all(sent, "z", split_axis=0, concat_axis=0, tiled=True)
    own = gather_y(both)
    blocks, own = ring_of_four(planes, along_x, 0, after=own)
    other = permute(own, lambda z, x, y, core: (z, x, y, core + 1))
    full, mine = local_call(arrange_kernel, [((4, 256, 640), half), ((256, 384), half)], place, own, other)
    left = pl.pallas_call(
        left_kernel,
        out_shape=jax.ShapeDtypeStruct((tiles, slots, 8 * width), half),
        in_specs=[SMEM, VMEM, VMEM],
        out_specs=VMEM,
        scratch_shapes=[pltpu.VMEM((8 * width, slots), half)],
        compiler_params=pltpu.CompilerParams(vmem_limit_bytes=32 * 2**20),
        cost_estimate=pl.CostEstimate(flops=0, bytes_accessed=4000000, transcendentals=0),
    )(place, own, other)
    (solved,) = local_call(
        solve_kernel, [((tiles, width, slots), half)], place, full, mine, *flat(blocks), flops=500000000
    )

    moved = permute(
        solved,
        lambda z, x, y, core: (
            z + y - 2,
            x + z // 2 + x % 2,
            2 * (z % 2) + x // 2,
            core,
        ),
    )
    rows, moved = lax.optimization_barrier((gather_y(solved), moved))
    lines, rows = ring_of_eight(moved, along_z, rows)
    rows = ring_of_four(rows, along_x, 0)
    kept, given = partial_cores(rows, lines)
    given = permute(given, lambda z, x, y, core: (z, x, y, core + 1))
    given, left = lax.optimization_barrier((given, left))
    cores = (kept + given).astype(half)
    pieces = [cores[0]] + [along_x(cores[step], step) for step in (1, 2, 3)]
    update = apply_cores([0], [pieces[0]], left)
    for step in (1, 3, 2):
        update = apply_cores([step], [pieces[step]], left, update)
    return jnp.swapaxes(solved, 1, 2), update


def solution(mesh):
    fine = Mesh(mesh.devices.reshape(SIZES), AXES)
    row, col = ("z", "x"), ("y", "core")
    placed = (P(row, None, col), P(row, None, col), P(row), P(row, col))
    return jax.shard_map(
        local,
        mesh=fine,
        in_specs=placed,
        out_specs=(P(row, None, col), P(row, col, None, None, None)),
        check_vma=False,
    )
```

```python
import functools

import jax
import jax.numpy as jnp
from jax import lax
from jax.experimental import pallas as pl
from jax.experimental.pallas import tpu as pltpu
from jax.sharding import Mesh, PartitionSpec as P

AXES = ("z", "x", "y", "core")
SIZES = (8, 4, 4, 2)


def permute(value, target):
    pairs = []
    for z in range(8):
        for x in range(4):
            for y in range(4):
                for core in range(2):
                    goal = [p % s for p, s in zip(target(z, x, y, core), SIZES)]
                    source = ((z * 4 + x) * 4 + y) * 2 + core
                    pairs.append((source, ((goal[0] * 4 + goal[1]) * 4 + goal[2]) * 2 + goal[3]))
    return lax.ppermute(value, AXES, pairs)


def along_x(value, step):
    return permute(value, lambda z, x, y, core: (z, x + step, y, core))


def ring_of_four(value, shift, dim, after=None):
    below, above = shift(value, 1), shift(value, -1)
    if after is not None:
        below, above, after = lax.optimization_barrier((below, above, after))
    half = value.shape[dim] // 2
    first = lax.slice_in_dim(below, 0, half, axis=dim)
    second = lax.slice_in_dim(above, half, value.shape[dim], axis=dim)
    gathered = [value, above, (shift(first, 1), shift(second, -1)), below]
    return gathered if after is None else (gathered, after)


def flat(blocks):
    return jax.tree.leaves(blocks)


def stacked(blocks, dim):
    return jnp.stack([jnp.concatenate(b, axis=dim) if isinstance(b, tuple) else b for b in blocks])


def along_y(value, step):
    return permute(value, lambda z, x, y, core: (z, x, y + step, core))


def gather_y(value):
    far, above, below = along_y(value, 2), along_y(value, -1), along_y(value, 1)
    return jnp.stack([value, above, far, below])


def along_z(value, step):
    return permute(value, lambda z, x, y, core: (z + step, x, y, core))


def ring_of_eight(value, shift, after):
    below, above = [value], [value]
    for step in range(3):
        near, far = shift(below[-1], 1), shift(above[-1], -1)
        below.append(near)
        above.append(far)
    half = value.shape[1] // 2
    first = shift(below[3][:, :half], 1)
    second = shift(above[3][:, half:], -1)
    across = jnp.concatenate([first, second], axis=1)
    return above + [across] + below[:0:-1], after


def partial_kernel(place, *refs):
    rows, lines, (kept, given, columns) = refs[:4], refs[4:12], refs[12:]
    first, core, mid = place[0], place[1], place[2]
    for far, line in enumerate(lines):
        at = lax.rem(first + far, 8)
        start = pl.multiple_of(320 * lax.rem(at, 4), 64)
        side = lax.rem(lax.div(at, 4) + core, 2)
        columns[side, pl.ds(start, 320), :] = jnp.concatenate([line[0], line[1]], axis=1)
    mine, others = columns[0].T, columns[1].T
    for step, row in enumerate(rows):
        near = [lax.rem(y + 4 - mid, 4) for y in range(4)]
        block = jnp.concatenate([jnp.concatenate([row[at, 0], row[at, 1]], axis=1) for at in near], axis=0)
        kept[step] = jnp.dot(mine, block, preferred_element_type=jnp.float32)
        given[step] = jnp.dot(others, block, preferred_element_type=jnp.float32).astype(given.dtype)


def partial_cores(rows, lines):
    rows = [jnp.concatenate(row, axis=0) if isinstance(row, tuple) else row for row in rows]
    z, x, y, core = (lax.axis_index(name).astype(jnp.int32) for name in AXES)
    first = z - 2 * ((x - 2 * (y % 2) - 2) % 4) - y // 2 - 2
    place = jnp.stack([first % 8, core, y])
    wide = 2 * rows[0].shape[-1]
    vmem = pl.BlockSpec(memory_space=pltpu.VMEM)
    return pl.pallas_call(
        partial_kernel,
        out_shape=[jax.ShapeDtypeStruct((4, wide, wide), dtype) for dtype in (jnp.float32, jnp.float32)],
        in_specs=[pl.BlockSpec(memory_space=pltpu.SMEM)] + [vmem] * 12,
        out_specs=(vmem, vmem),
        scratch_shapes=[pltpu.VMEM((2, 1280, wide), rows[0].dtype)],
        compiler_params=pltpu.CompilerParams(vmem_limit_bytes=32 * 2**20),
        cost_estimate=pl.CostEstimate(flops=1400000000, bytes_accessed=6000000, transcendentals=0),
    )(place, *rows, *lines)


def apply_kernel(count, place, left, *refs):
    pieces = refs[:count]
    out, product, sems = refs[-3:]
    copies = []
    for number, cores in enumerate(pieces):
        for part in range(5):
            span = pl.ds(512 * part, 512)
            for tile in range(2):
                block = jnp.dot(
                    cores[:, tile * 128:(tile + 1) * 128], left[tile, :, span], preferred_element_type=jnp.float32
                ).astype(out.dtype)
                for column in range(2):
                    product[number, tile, column, :, span] = block[128 * column:128 * column + 128]
                copies.append(
                    pltpu.make_async_copy(
                        product.at[number, tile, :, :, span],
                        out.at[tile, 0, pl.ds(2 * place[number], 2), :, span],
                        sems.at[number, part, tile],
                    )
                )
                copies[-1].start()
    for copy in copies:
        copy.wait()


def apply_cores(steps, pieces, left, so_far=None):
    tiles, slots, order = left.shape
    _, x, y, core = (lax.axis_index(name).astype(jnp.int32) for name in AXES)
    place = jnp.stack([(x - 2 * (y % 2) - 2 * core - step) % 4 for step in steps])
    count = len(steps)
    earlier = [] if so_far is None else [so_far]
    return pl.pallas_call(
        functools.partial(apply_kernel, count),
        out_shape=jax.ShapeDtypeStruct((tiles, 1, 8, slots, order), jnp.bfloat16),
        in_specs=[SMEM] + [VMEM] * (1 + count) + [pl.BlockSpec(memory_space=pl.ANY)] * len(earlier),
        out_specs=pl.BlockSpec(memory_space=pl.ANY),
        input_output_aliases={2 + count: 0} if earlier else {},
        scratch_shapes=[pltpu.VMEM((count, tiles, 2, slots, order), jnp.bfloat16), pltpu.SemaphoreType.DMA((count, 5, 2))],
        compiler_params=pltpu.CompilerParams(vmem_limit_bytes=32 * 2**20),
        cost_estimate=pl.CostEstimate(flops=350000000 * count, bytes_accessed=4000000 * count, transcendentals=0),
    )(place, left, *pieces, *earlier)


VMEM = pl.BlockSpec(memory_space=pltpu.VMEM)
SMEM = pl.BlockSpec(memory_space=pltpu.SMEM)


def local_call(kernel, shapes, *operands, flops=0, bytes_accessed=4000000):
    outs = [jax.ShapeDtypeStruct(shape, dtype) for shape, dtype in shapes]
    return pl.pallas_call(
        kernel,
        out_shape=outs,
        in_specs=[SMEM] + [VMEM] * (len(operands) - 1),
        out_specs=[VMEM] * len(outs),
        compiler_params=pltpu.CompilerParams(vmem_limit_bytes=32 * 2**20),
        cost_estimate=pl.CostEstimate(flops=flops, bytes_accessed=bytes_accessed, transcendentals=0),
    )(*operands)


def pack_kernel(place, inverse, out):
    exact = inverse[...]
    rounded = exact.astype(jnp.bfloat16).astype(jnp.float32)
    rows = lax.broadcasted_iota(jnp.int32, exact.shape, 0) + place[0]
    cols = lax.broadcasted_iota(jnp.int32, exact.shape, 1) + place[1]
    rest = jnp.sum(jnp.where(rows == cols, exact - rounded, 0.0), axis=0, keepdims=True)
    rests = [rest[:, at:at + 64] for at in range(0, 320, 64)]
    tail = jnp.concatenate([rounded[48:, 256:]] + rests + [jnp.zeros((11, 64), jnp.float32)], axis=0)
    ends = jnp.concatenate([rounded[:48, 256:], tail], axis=1)
    packed = jnp.concatenate([rounded[:, :128], rounded[:, 128:256], ends], axis=0).astype(jnp.bfloat16)
    for copy in range(8):
        out[copy] = packed


def arrange_kernel(place, own, other, full, mine):
    x, mid = place[0], place[1]
    for step in range(4):
        start = pl.multiple_of(80 * lax.rem(x + step, 4), 16)
        low, high = [], []
        for side in (own, other):
            for y in range(4):
                near = lax.rem(y + 4 - mid, 4)
                part = jnp.concatenate([side[near, 2 + tile, pl.ds(start, 80), :] for tile in range(2)], axis=1)
                low.append(part[:48])
                high.append(part[48:])
        full[step] = jnp.concatenate(low + high, axis=0).T
    here = jnp.concatenate([own[0, 2], own[0, 3]], axis=1)
    mine[...] = jnp.concatenate([here, jnp.zeros((64, 256), here.dtype)], axis=0).T


def left_kernel(place, own, other, left, rows):
    mid, core = place[1], place[2]
    for tile in range(2):
        for side, at in ((own, core), (other, 1 - core)):
            for near in range(4):
                y = lax.rem(mid + near, 4)
                rows[pl.ds(pl.multiple_of(640 * y + 320 * at, 64), 320), :] = side[near, tile]
        left[tile] = rows[...].T


def solve_kernel(place, full, mine, here, above, first, second, below, out):
    core = place[2]
    order = [2 * y + core for y in range(4)] + [2 * y + 1 - core for y in range(4)]
    wide = jnp.zeros((256, 256), jnp.float32)
    lows = jnp.zeros((256, 128), jnp.float32)
    highs = jnp.zeros((256, 128), jnp.float32)
    rest = jnp.zeros((16, 128), jnp.float32)
    for step in range(4):
        if step == 2:
            blocks = [(first if at % 4 < 2 else second, order[at] - at % 4 // 2 * 4) for at in range(8)]
        else:
            blocks = [((here, above, None, below)[step], at) for at in order]
        parts = [
            jnp.concatenate(
                [ref[at, low:low + 48, :] for ref, at in blocks] + [ref[at, low + 48:low + 80, :] for ref, at in blocks],
                axis=0,
            )
            for low in (0, 80)
        ]
        ends = jnp.concatenate([ref[at, 160:208, :] for ref, at in blocks], axis=0)
        tails = jnp.concatenate([ref[at, 160:192, :] for ref, at in blocks], axis=0)
        rows = full[step]
        wide += jnp.dot(rows, jnp.concatenate(parts, axis=1), preferred_element_type=jnp.float32)
        lows += jnp.dot(rows[:, :384], ends, preferred_element_type=jnp.float32)
        highs += jnp.dot(rows[:, 384:], tails, preferred_element_type=jnp.float32)
        for ref, at in blocks:
            rest += ref[at, 192:208, :].astype(jnp.float32)
    own = mine[...].astype(jnp.float32)
    rest = rest[:, 64:]
    wide += own[:, :256] * jnp.concatenate([rest[at:at + 1] for at in range(4)], axis=1)
    lows += own[:, 256:] * jnp.concatenate([rest[4:5], jnp.zeros((1, 64), jnp.float32)], axis=1)
    ends = lows.T[:64] + highs.T[64:]
    total = jnp.concatenate([wide.T, ends], axis=0)
    slot = lax.broadcasted_iota(jnp.int32, (320, 128), 1)
    for tile in range(2):
        part = total[:, tile * 128:(tile + 1) * 128]
        out[tile] = jnp.where(slot < place[3 + tile], part, 0.0).astype(out.dtype)


def local(u_panel, v_panel, ranks, inverse_t):
    tiles, slots, width = v_panel.shape
    depth = inverse_t.shape[0]
    z, x, y, core = (lax.axis_index(name).astype(jnp.int32) for name in AXES)
    place = jnp.stack([x, y, core, ranks[0], ranks[1], z])
    corner = jnp.stack([depth * (z * 4 + x), width * (y * 2 + core)])
    half = jnp.bfloat16

    (sent,) = local_call(pack_kernel, [((8, 208, 128), half)], corner, inverse_t)
    both = jnp.concatenate([jnp.swapaxes(u_panel, 1, 2), jnp.swapaxes(v_panel, 1, 2)], axis=0)
    both, sent = lax.optimization_barrier((both, sent))
    planes = lax.all_to_all(sent, "z", split_axis=0, concat_axis=0, tiled=True)
    own = gather_y(both)
    blocks, own = ring_of_four(planes, along_x, 0, after=own)
    other = permute(own, lambda z, x, y, core: (z, x, y, core + 1))
    full, mine = local_call(arrange_kernel, [((4, 256, 640), half), ((256, 384), half)], place, own, other)
    left = pl.pallas_call(
        left_kernel,
        out_shape=jax.ShapeDtypeStruct((tiles, slots, 8 * width), half),
        in_specs=[SMEM, VMEM, VMEM],
        out_specs=VMEM,
        scratch_shapes=[pltpu.VMEM((8 * width, slots), half)],
        compiler_params=pltpu.CompilerParams(vmem_limit_bytes=32 * 2**20),
        cost_estimate=pl.CostEstimate(flops=0, bytes_accessed=4000000, transcendentals=0),
    )(place, own, other)
    (solved,) = local_call(
        solve_kernel, [((tiles, width, slots), half)], place, full, mine, *flat(blocks), flops=500000000
    )

    moved = permute(
        solved,
        lambda z, x, y, core: (
            z + y - 2,
            x + z // 2 + x % 2,
            2 * (z % 2) + x // 2,
            core,
        ),
    )
    rows, moved = lax.optimization_barrier((gather_y(solved), moved))
    lines, rows = ring_of_eight(moved, along_z, rows)
    rows = ring_of_four(rows, along_x, 0)
    kept, given = partial_cores(rows, lines)
    given = permute(given, lambda z, x, y, core: (z, x, y, core + 1))
    cores = (kept + given.astype(jnp.float32)).astype(half)
    pieces = [cores[0]] + [along_x(cores[step], step) for step in (1, 2, 3)]
    update = apply_cores([0], [pieces[0]], left)
    for step in (2, 1, 3):
        update = apply_cores([step], [pieces[step]], left, update)
    return jnp.swapaxes(solved, 1, 2), update


def solution(mesh):
    fine = Mesh(mesh.devices.reshape(SIZES), AXES)
    row, col = ("z", "x"), ("y", "core")
    placed = (P(row, None, col), P(row, None, col), P(row), P(row, col))
    return jax.shard_map(
        local,
        mesh=fine,
        in_specs=placed,
        out_specs=(P(row, None, col), P(row, col, None, None, None)),
        check_vma=False,
    )
```
